256 devices in a mesh: tile: 64 (over z_hi, y, x), lev: 4 (over z_lo, core).
Axes of the slice: x: 4, y: 4, z: 8 (z_hi: 4, z_lo: 2; z = z_hi * 2 + z_lo), core: 2. Of those that a mesh axis runs over, the one named last changes fastest.
Arguments:
- control: float32 [20, 128, 768, 128], P(None, 'lev', 'tile'), may hold values from -6 to 6
- ensemble: bfloat16 [20, 128, 768, 128], P(None, 'lev', 'tile'), may hold values from -6 to 6
- coupling_x: float32 [768, 128], P('tile'), may hold values from 0.16 to 0.245
- coupling_y: float32 [128], replicated, may hold values from 0.16 to 0.245
- vertical_loc: bfloat16 [128, 128], replicated
- obs_cells: int32 [4096, 32], P('tile'), may hold values from 0 to 1535, as said below
- obs_counts: int32 [4096], P('tile'), may hold values from 8 to 32, as said below
- obs_values: float32 [4096, 32, 128], P('tile', None, 'lev'), may hold values from -6 to 6
Outputs:
- increment: float32 [128, 768, 128], P('lev', 'tile')
- gradient: float32 [20, 128, 768, 128], P(None, 'lev', 'tile')
The draws below stay inside these ranges and needn't reach their ends.
Inputs may be any that keep to these rules, and one draw needn't show every extreme that they name: `obs_cells`: each row holds owner-local cells of one owner, in rising order. The live slots of a row are its first obs_counts entries; in every draw some owners receive 32 live slots from every device.
All inputs are finite; a program needn't handle non-finite values.
Results may differ from the reference program's by a relative error of at most 0.0029.
Values may be sent and summed in bfloat16 or wider, within the bound.
No kernel may reach another device: no remote copies, remote signals or barrier semaphores. Data moves between devices by JAX's collectives and lax.ppermute only.
A program may use at most 64 MiB of HBM per device.

```python
import math
import jax
import jax.numpy as jnp
from jax import lax

M = 20
L = 128
CX = 12
CY = 128
STEPS = 4
CAP = 32
OWNERS = 64
NX = 768
OBS_ROWS = 4096


def draw_control(key, part):
    normal_part = jax.random.normal(key, (M, L, NX, CY), jnp.float32)
    return jnp.clip(normal_part, -6.0, 6.0)


def draw_vertical_loc(key, part):
    levels = jnp.arange(L, dtype=jnp.float32)
    distance = (levels[:, None] - levels[None, :]) / (L / 1.5)
    factor = jax.random.uniform(key, (L, L), jnp.float32, 0.5, 1.5)
    return (0.5 * factor * (0.15 + jnp.exp(-distance * distance))).astype(jnp.bfloat16)


def draw_obs_cells(key, part):
    raw_cells = jax.random.randint(key, (OBS_ROWS, CAP), 0, CX * CY, dtype=jnp.int32)
    return jnp.sort(raw_cells, axis=1)


def draw_obs_counts(key, part):
    owner = jnp.arange(OBS_ROWS, dtype=jnp.int32) % OWNERS
    shuffled = jax.random.permutation(jax.random.fold_in(key, 7), OWNERS)
    busiest = shuffled[:max(1, OWNERS // 8)]
    is_busy = jnp.any(owner[:, None] == busiest[None, :], axis=1)
    base_count = jax.random.randint(jax.random.fold_in(key, 3), (OBS_ROWS,), CAP // 4, CAP // 2 + 1, dtype=jnp.int32)
    return jnp.where(is_busy, jnp.int32(CAP), base_count).astype(jnp.int32)


def level_of(own_key, shape, pieces, smallest, high):
    level, own = 1.0, jax.random.fold_in(own_key, 6)
    for dim, blocks in pieces:
        heights = jnp.exp(jax.random.uniform(jax.random.fold_in(own, dim), (blocks,), jnp.float32, smallest / len(pieces), high / len(pieces)))
        level = level * jnp.repeat(heights, shape[dim] // blocks).reshape([-1 if axis == dim else 1 for axis in range(len(shape))])
    return level


def gaussian(key, extent, spread, most, shards=(), kind=jnp.bfloat16):
    result = jax.random.normal(key, extent, jnp.float32) * spread
    if len(shards) > 0:
        result = level_of(key, extent, shards, -0.22, 0.18) * result
    return jnp.clip(result, min=-most, max=most).astype(kind)


def setup_inputs(seed: int = 0) -> dict:
    key_list = jax.random.split(jax.random.key(seed), 9)
    control = draw_control(jax.random.fold_in(key_list[8], 71), 0)
    ensemble = gaussian(key_list[1], (M, L, NX, CY), 1.0, 6.0, ((1, 4), (2, 64)))
    coupling_x = jnp.clip(jnp.exp(math.log(0.245) - 0.42608444 * jax.random.uniform(key_list[2], (NX, CY), jnp.float32) ** level_of(key_list[2], (NX, CY), ((0, 64),), -0.2, 0.2)), 0.16, 0.245)
    coupling_y = jnp.clip(jnp.exp(jax.random.uniform(key_list[3], (CY,), jnp.float32, math.log(0.16), math.log(0.245))), 0.16, 0.245)
    vertical_loc = draw_vertical_loc(jax.random.fold_in(key_list[8], 71), 0)
    obs_cells = draw_obs_cells(jax.random.fold_in(key_list[8], 71), 0)
    obs_counts = draw_obs_counts(jax.random.fold_in(key_list[8], 71), 0)
    obs_values = gaussian(key_list[7], (OBS_ROWS, CAP, L), 1.0, 6.0, ((0, 64), (2, 4)), jnp.float32)
    return dict(control=control, ensemble=ensemble, coupling_x=coupling_x, coupling_y=coupling_y, vertical_loc=vertical_loc, obs_cells=obs_cells, obs_counts=obs_counts, obs_values=obs_values)


def sweep_across(middle, coupling_y):
    differ = middle[..., 1:] - middle[..., :-1]
    fluxes = coupling_y[:-1] * differ
    zeros_col = jnp.zeros_like(middle[..., :1])
    return jnp.concatenate([fluxes, zeros_col], -1) - jnp.concatenate([zeros_col, fluxes], -1)


def diffuse(field, coupling_x, coupling_y):
    behind_x = jnp.roll(coupling_x, 1, 0)
    for step in range(STEPS):
        forward_col = jnp.roll(field, -1, -2)
        backward_col = jnp.roll(field, 1, -2)
        field = field + (coupling_x * (forward_col - field) - behind_x * (field - backward_col)) + sweep_across(field, coupling_y)
    return field


def reference(control, ensemble, coupling_x, coupling_y, vertical_loc, obs_cells, obs_counts, obs_values):
    slot_index = lax.broadcasted_iota(jnp.int32, obs_cells.shape, 1)
    live = slot_index < obs_counts[:, None]
    masked = jnp.where(live[..., None], obs_values, jnp.float32(0.0))
    owner = (jnp.arange(OBS_ROWS, dtype=jnp.int32) % OWNERS).astype(jnp.int32)
    flat_ids = (owner[:, None] * (CX * CY) + obs_cells).astype(jnp.int32)
    summed = jax.ops.segment_sum(masked.reshape(-1, L), flat_ids.reshape(-1), num_segments=NX * CY)
    obs_grad = summed.T.reshape(L, NX, CY)

    def forward_member(carry, pair):
        member_ctl, member_ens = pair
        smooth = diffuse(member_ctl, coupling_x, coupling_y).astype(jnp.bfloat16)
        localized = jnp.dot(vertical_loc, smooth.reshape(L, -1), preferred_element_type=jnp.float32).reshape(L, NX, CY)
        return carry + member_ens.astype(jnp.float32) * localized, None

    increment, unused = lax.scan(forward_member, jnp.zeros((L, NX, CY), jnp.float32), (control, ensemble))

    def adjoint_member(pair):
        member_ctl, member_ens = pair
        weighted = (member_ens.astype(jnp.float32) * obs_grad).astype(jnp.bfloat16)
        returned = jnp.dot(vertical_loc.T, weighted.reshape(L, -1), preferred_element_type=jnp.float32).reshape(L, NX, CY)
        return member_ctl + diffuse(returned, coupling_x, coupling_y)

    gradient = lax.map(adjoint_member, (control, ensemble))
    return increment, gradient
```

```python
import functools

import jax
import jax.numpy as jnp
from jax import lax
from jax.experimental import pallas as pl
from jax.experimental.pallas import tpu as pltpu
from jax.sharding import PartitionSpec as P

STEPS = 4
W = STEPS
PLANE = 16


def chunks_of(half):
    sizes = [half - half // 2, half // 2]
    out, at = [], 0
    for s in sizes:
        if s:
            out.append((at, s))
            at += s
    return out


def permute(x, route):
    tiles, levs = lax.axis_size("tile"), lax.axis_size("lev")
    pairs = []
    for t in range(tiles):
        for j in range(levs):
            to = route(t, j)
            if to is not None:
                pairs.append((t * levs + j, (to[0] % tiles) * levs + to[1]))
    return lax.ppermute(x, ("tile", "lev"), pairs)


def flip_core(x):
    return permute(x, lambda t, j: (t, j ^ 1))


def flip_chip(x):
    return permute(x, lambda t, j: (t, j ^ 2))


def up(x):
    return permute(x, lambda t, j: (t + 1, j))


def down(x):
    return permute(x, lambda t, j: (t - 1, j))


def up_near(x):
    def route(t, j):
        if t % PLANE != PLANE - 1:
            return (t + 1, j)
        return (t + 1, j ^ 2) if j >= 2 else None

    return permute(x, route)


def down_near(x):
    def route(t, j):
        if t % PLANE != 0:
            return (t - 1, j)
        return (t - 1, j ^ 2) if j < 2 else None

    return permute(x, route)


def relay(x):
    def route(t, j):
        if t % PLANE == 0 and j < 2:
            return (t, j ^ 2)
        if t % PLANE == PLANE - 1 and j >= 2:
            return (t, j ^ 2)
        return None

    return permute(x, route)


def across(u, cy):
    n = u.shape[-1]
    f = cy * (pltpu.roll(u, n - 1, u.ndim - 1) - u)
    return f - pltpu.roll(f, 1, u.ndim - 1)


def sweep(u_ref, lo, hi, cx_ref, cy, emit):
    count = u_ref.shape[0]
    cur = u_ref[lo]
    before = cx_ref[lo - 1 : lo, :] * (cur - u_ref[lo - 1]) if lo > 0 else None
    for x in range(lo, hi + 1):
        nxt = u_ref[x + 1] if x + 1 < count else None
        flux = cx_ref[x : x + 1, :] * (nxt - cur) if nxt is not None else None
        new = cur + across(cur, cy)
        if flux is not None:
            new = new + flux
        if before is not None:
            new = new - before
        emit(x, new)
        cur, before = nxt, flux


def smooth_kernel(c_ref, ctl_ref, cx_ref, cy_ref, out_ref, u_ref):
    cols = ctl_ref.shape[1]
    cy = cy_ref[...]
    zero = jnp.zeros(u_ref.shape[1:], u_ref.dtype)
    for x in range(W):
        u_ref[x] = zero
        u_ref[W + cols + x] = zero
    for x in range(cols):
        u_ref[W + x] = ctl_ref[0, x]

    def keep(x, v):
        u_ref[x] = v

    def give(x, v):
        out_ref[0, x] = v.astype(out_ref.dtype)

    for step in range(1, STEPS + 1):
        sweep(u_ref, W - step, W + cols - 1 + step, cx_ref, cy, keep if step < STEPS else give)


def smooth_call(core, control, cxe, cyz):
    m, cols, lev, cy = control.shape
    half = m // 2
    ext = cols + 2 * W
    return pl.pallas_call(
        smooth_kernel,
        grid_spec=pltpu.PrefetchScalarGridSpec(
            num_scalar_prefetch=1,
            grid=(m,),
            in_specs=[
                pl.BlockSpec((1, cols, lev, cy), lambda i, c: (lax.rem(i + half * c[0], m), 0, 0, 0)),
                pl.BlockSpec((ext, cy), lambda i, c: (0, 0)),
                pl.BlockSpec((1, cy), lambda i, c: (0, 0)),
            ],
            out_specs=pl.BlockSpec((1, ext, lev, cy), lambda i, c: (i, 0, 0, 0)),
            scratch_shapes=[pltpu.VMEM((ext, lev, cy), jnp.float32)],
        ),
        out_shape=jax.ShapeDtypeStruct((m, ext, lev, cy), jnp.bfloat16),
        compiler_params=pltpu.CompilerParams(vmem_limit_bytes=32 * 2**20),
        cost_estimate=pl.CostEstimate(flops=80 * control.size, bytes_accessed=8 * control.size, transcendentals=0),
        name="smooth",
    )(core, control, cxe, cyz)


def scatter_kernel(vals_ref, cells_ref, out_ref):
    cols, lev, cy = out_ref.shape
    groups = vals_ref.shape[1] // lev
    rows = vals_ref.shape[0]
    vt = vals_ref[...].T
    high = vt.astype(jnp.bfloat16)
    low = (vt - high.astype(jnp.float32)).astype(jnp.bfloat16)
    lane = lax.broadcasted_iota(jnp.int32, (rows, cy), 1)
    total = [jnp.zeros((2 * lev, cy), jnp.float32) for _ in range(cols)]
    for a in range(groups):
        part = slice(a * lev, (a + 1) * lev)
        both = jnp.concatenate([high[part], low[part]], 0)
        cell = jnp.broadcast_to(cells_ref[:, a : a + 1], (rows, cy)).astype(jnp.int32) - lane
        for x in range(cols):
            hot = jnp.where(cell == x * cy, jnp.float32(1), jnp.float32(0)).astype(jnp.bfloat16)
            total[x] = total[x] + jnp.dot(both, hot, preferred_element_type=jnp.float32)
    for x in range(cols):
        out_ref[x] = total[x][:lev] + total[x][lev:]


def scatter_call(vals, cells, cols, lev, cy):
    return pl.pallas_call(
        scatter_kernel,
        out_shape=jax.ShapeDtypeStruct((cols, lev, cy), jnp.float32),
        in_specs=[pl.BlockSpec(memory_space=pltpu.VMEM)] * 2,
        out_specs=pl.BlockSpec(memory_space=pltpu.VMEM),
        compiler_params=pltpu.CompilerParams(vmem_limit_bytes=32 * 2**20),
        cost_estimate=pl.CostEstimate(flops=2**30, bytes_accessed=2**20, transcendentals=0),
        name="scatter",
    )(vals, cells)


def member_kernel(
    core_ref, own_ref, far_ref, left_ref, right_ref, s0_ref, s1_ref, g_ref, vf_ref, vt_ref, cx_ref, cy_ref,
    ctl_ref, part_ref, _grad, grad_ref, other_ref, inc_ref, u_ref,
):
    cols, lev, _ = grad_ref.shape[1:]
    ext = cols + 2 * W
    cy = cy_ref[...]

    @pl.when(pl.program_id(0) == 0)
    def _():
        inc_ref[...] = part_ref[...]

    def block(b, x):
        if x < W:
            return left_ref[b, 0, x]
        if x >= W + cols:
            return right_ref[b, 0, x - W - cols]
        return own_ref[b, 0, x - W] if b < 2 else far_ref[b - 2, 0, x - W]

    for x in range(0, ext, 2):
        weighted, smooth = [], []
        for y in (x, x + 1):
            weighted.append(
                jnp.concatenate([(block(b, y).astype(jnp.float32) * g_ref[b, y]).astype(jnp.bfloat16) for b in range(4)], 0)
            )
            smooth.append(jnp.concatenate([s0_ref[0, y], s1_ref[0, y]], 0))
        back = jnp.dot(vt_ref[...], jnp.concatenate(weighted, 1), preferred_element_type=jnp.float32)
        local = jnp.dot(vf_ref[...], jnp.concatenate(smooth, 1), preferred_element_type=jnp.float32)
        width = back.shape[1] // 2
        for i, y in enumerate((x, x + 1)):
            u_ref[y] = back[:, i * width : (i + 1) * width]
            for b in range(4):
                inc_ref[b, y] += block(b, y).astype(jnp.float32) * local[b * lev : (b + 1) * lev, i * width : (i + 1) * width]

    def keep(x, v):
        u_ref[x] = v

    def give(x, v):
        grad_ref[0, x - W] = ctl_ref[0, x - W] + v[:lev]
        other_ref[0, x - W] = v[lev:]

    for step in range(1, STEPS + 1):
        sweep(u_ref, step, ext - 1 - step, cx_ref, cy, keep if step < STEPS else give)


def member_call(core, at, own, far, left, right, s0, s1, g, vf, vt, cxe, cyz, control, part, grad):
    _, c, cols, lev, cy = own.shape
    m = control.shape[0]
    half = m // 2
    ext = cols + 2 * W
    first = grad is None
    whole = pl.BlockSpec((4, ext, lev, cy), lambda i, k: (0, 0, 0, 0))
    pair = pl.BlockSpec((2, 1, cols, lev, cy), lambda i, k: (0, i, 0, 0, 0))
    halo = pl.BlockSpec((4, 1, W, lev, cy), lambda i, k: (0, i, 0, 0, 0))
    spread = pl.BlockSpec((1, ext, lev, cy), lambda i, k: (at + i, 0, 0, 0))
    moved = pl.BlockSpec((1, ext, lev, cy), lambda i, k: (at + i, 0, 0, 0))
    mine = pl.BlockSpec((1, cols, lev, cy), lambda i, k: (k[0] * half + at + i, 0, 0, 0))

    def flat(shape):
        return pl.BlockSpec(shape, lambda i, k: (0,) * len(shape))

    in_specs = [pair, pair, halo, halo, spread, moved, whole, flat(vf.shape), flat(vt.shape), flat(cxe.shape), flat(cyz.shape), mine, whole]
    args = [own, far, left, right, s0, s1, g, vf, vt, cxe, cyz, control, part]
    body = member_kernel
    aliases = {}
    if first:
        body = functools.partial(_no_grad, member_kernel)
    else:
        in_specs.append(pl.BlockSpec(memory_space=pl.ANY))
        args.append(grad)
        aliases = {len(args): 0}
    return pl.pallas_call(
        body,
        grid_spec=pltpu.PrefetchScalarGridSpec(
            num_scalar_prefetch=1,
            grid=(c,),
            in_specs=in_specs,
            out_specs=[mine, pl.BlockSpec((1, cols, lev, cy), lambda i, k: (i, 0, 0, 0)), whole],
            scratch_shapes=[pltpu.VMEM((ext, 2 * lev, cy), jnp.float32)],
        ),
        out_shape=[
            jax.ShapeDtypeStruct(control.shape, jnp.float32),
            jax.ShapeDtypeStruct((c, cols, lev, cy), jnp.float32),
            jax.ShapeDtypeStruct(part.shape, jnp.float32),
        ],
        input_output_aliases=aliases,
        compiler_params=pltpu.CompilerParams(vmem_limit_bytes=40 * 2**20),
        cost_estimate=pl.CostEstimate(flops=c * 2**28, bytes_accessed=c * 2**20, transcendentals=0),
        name="members",
    )(core, *args)


def _no_grad(body, *refs):
    body(*refs[:14], None, *refs[14:])


def finish_kernel(_core, r_ref, ctl_ref, _grad, out_ref):
    out_ref[...] = ctl_ref[...] + r_ref[...]


def finish_call(core, at, r, control, grad):
    c, cols, lev, cy = r.shape
    half = control.shape[0] // 2
    theirs = pl.BlockSpec((1, cols, lev, cy), lambda i, k: ((1 - k[0]) * half + at + i, 0, 0, 0))
    return pl.pallas_call(
        finish_kernel,
        grid_spec=pltpu.PrefetchScalarGridSpec(
            num_scalar_prefetch=1,
            grid=(c,),
            in_specs=[pl.BlockSpec((1, cols, lev, cy), lambda i, k: (i, 0, 0, 0)), theirs, pl.BlockSpec(memory_space=pl.ANY)],
            out_specs=theirs,
        ),
        out_shape=jax.ShapeDtypeStruct(control.shape, jnp.float32),
        input_output_aliases={3: 0},
        compiler_params=pltpu.CompilerParams(vmem_limit_bytes=16 * 2**20),
        cost_estimate=pl.CostEstimate(flops=r.size, bytes_accessed=12 * r.size, transcendentals=0),
        name="finish",
    )(core, r, control, grad)


def local(control, ensemble, coupling_x, coupling_y, vertical_loc, obs_cells, obs_counts, obs_values):
    m, lev, cols, cy = control.shape
    half = m // 2
    tile, j = lax.axis_index("tile"), lax.axis_index("lev")
    core, chip = j % 2, j // 2
    core_arg = core.astype(jnp.int32).reshape(1)
    control = jnp.transpose(control, (0, 2, 1, 3))
    ens = jnp.transpose(ensemble, (0, 2, 1, 3))

    slot = lax.broadcasted_iota(jnp.int32, obs_cells.shape, 1)
    live = slot < obs_counts[:, None]
    masked = jnp.where(live[..., None], obs_values, jnp.float32(0.0))
    rows, cap = obs_cells.shape
    flat = masked.reshape(rows, cap * lev)
    message = jnp.concatenate(
        [flat, obs_cells.astype(jnp.float32), jnp.zeros((rows, (-cap * (lev + 1)) % 128), jnp.float32)], 1
    )

    mine = jnp.where(core == 0, ens[:half], ens[half:])
    other = jnp.where(core == 0, ens[half:], ens[:half])
    beside = flip_core(other)
    plan = chunks_of(half)
    owns = [jnp.stack([mine[a : a + c], beside[a : a + c]]) for a, c in plan]
    fars = [flip_chip(o) for o in owns]

    got = lax.all_to_all(message, "tile", split_axis=0, concat_axis=0, tiled=True)

    before = up(coupling_x[cols - W :])
    after = down(coupling_x[:W])
    cxe = jnp.concatenate([before, coupling_x, after], 0)
    cyz = jnp.where(lax.broadcasted_iota(jnp.int32, (1, cy), 1) < cy - 1, coupling_y[None], jnp.float32(0.0))

    v = vertical_loc
    v = jnp.where(chip == 0, v, jnp.roll(v, (2 * lev, 2 * lev), (0, 1)))
    v6 = v.reshape(2, 2, lev, 2, 2, lev)
    v = jnp.where(core == 0, v6, v6[:, ::-1, :, :, ::-1, :]).reshape(4 * lev, 4 * lev)
    vf = v[:, : 2 * lev]
    vt = v[:, : 2 * lev].T

    smooth = smooth_call(core_arg, control, cxe, cyz)
    smooth_beside = flip_core(smooth[half:])

    vals = got[:, : cap * lev].reshape(rows * cap * lev // 128, 128)
    cells = got[:, cap * lev : cap * (lev + 1)].reshape(vals.shape[0], -1)
    g_own = scatter_call(vals, cells, cols, lev, cy)
    g_own = jnp.concatenate([up(g_own[cols - W :]), g_own, down(g_own[:W])], 0)
    g_far = flip_chip(g_own)
    g_pair = jnp.stack([g_own, g_far])
    g_beside = flip_core(g_pair)
    g = jnp.stack([g_own, g_beside[0], g_far, g_beside[1]])

    low_edge, high_edge = tile % PLANE == 0, tile % PLANE == PLANE - 1
    part = jnp.zeros((4, cols + 2 * W, lev, cy), jnp.float32)
    grad = None
    returned = []
    for (at, c), own, far in zip(plan, owns, fars):
        last = (own[:, :, cols - W :], far[:, :, cols - W :])
        head = (own[:, :, :W], far[:, :, :W])

        def ordered(swap, pair):
            return jnp.concatenate([jnp.where(swap, pair[1], pair[0]), jnp.where(swap, pair[0], pair[1])], 0)

        left = up_near(ordered(high_edge, last))
        right = down_near(ordered(low_edge, head))
        edge = jnp.where(low_edge, left, right)
        again = relay(jnp.concatenate([edge[2:], edge[:2]], 0))
        left = jnp.where(low_edge & (chip == 1), again, left)
        right = jnp.where(high_edge & (chip == 0), again, right)
        grad, r, part = member_call(
            core_arg, at, own, far, left, right, smooth, smooth_beside, g, vf, vt, cxe, cyz, control, part, grad
        )
        returned.append(flip_core(r))
    for (at, c), r in zip(plan, returned):
        grad = finish_call(core_arg, at, r, control, grad)

    pair = part[::2] + flip_core(part[1::2])
    total = pair[0] + flip_chip(pair[1])
    edge_low = up(total[W + cols :])
    edge_high = down(total[:W])
    middle = total[W : W + cols]
    inc = jnp.concatenate([middle[:W] + edge_low, middle[W : cols - W], middle[cols - W :] + edge_high], 0)
    return jnp.transpose(inc, (1, 0, 2)), jnp.transpose(grad, (0, 2, 1, 3))


def solution(mesh):
    placed = (
        P(None, "lev", "tile", None),
        P(None, "lev", "tile", None),
        P("tile", None),
        P(),
        P(),
        P("tile", None),
        P("tile"),
        P("tile", None, "lev"),
    )
    return jax.shard_map(
        local,
        mesh=mesh,
        in_specs=placed,
        out_specs=(P("lev", "tile", None), P(None, "lev", "tile", None)),
        check_vma=False,
    )
```

```python
import functools

import jax
import jax.numpy as jnp
from jax import lax
from jax.experimental import pallas as pl
from jax.experimental.pallas import tpu as pltpu
from jax.sharding import PartitionSpec as P

STEPS = 4
W = STEPS
PLANE = 16
COST = pl.CostEstimate(flops=1, bytes_accessed=1, transcendentals=0)


def chunks_of(half):
    sizes = [half - 2 * (2 * half // 5), 2 * half // 5, 2 * half // 5]
    out, at = [], 0
    for s in sizes:
        if s:
            out.append((at, s))
            at += s
    return out


def permute(x, route):
    tiles, levs = lax.axis_size("tile"), lax.axis_size("lev")
    pairs = []
    for t in range(tiles):
        for j in range(levs):
            to = route(t, j)
            if to is not None:
                pairs.append((t * levs + j, (to[0] % tiles) * levs + to[1]))
    return lax.ppermute(x, ("tile", "lev"), pairs)


def flip_core(x):
    return permute(x, lambda t, j: (t, j ^ 1))


def flip_chip(x):
    return permute(x, lambda t, j: (t, j ^ 2))


def swap_first(x):
    return permute(x, lambda t, j: (t + 1 if t % 2 == 0 else t - 1, j))


def swap_second(x):
    return permute(x, lambda t, j: (t - 1 if t % 2 == 0 else t + 1, j))


def swap_second_near(x):
    def route(t, j):
        to = t - 1 if t % 2 == 0 else t + 1
        if t % PLANE == 0:
            return (to, j ^ 2) if j < 2 else None
        if t % PLANE == PLANE - 1:
            return (to, j ^ 2) if j >= 2 else None
        return (to, j)

    return permute(x, route)


def beside_tile(even, top, bottom):
    a = swap_first(jnp.where(even, top, bottom))
    b = swap_second(jnp.where(even, bottom, top))
    return jnp.where(even, b, a), jnp.where(even, a, b)


def relay(x):
    def route(t, j):
        if (t % PLANE == 0 and j < 2) or (t % PLANE == PLANE - 1 and j >= 2):
            return (t, j ^ 2)
        return None

    return permute(x, route)


def reach(x):
    def route(t, j):
        if t % PLANE == PLANE - 1 and j >= 2:
            return (t + 1, j)
        if t % PLANE == 0 and j < 2:
            return (t - 1, j)
        return None

    return permute(x, route)


def sweep(u_ref, lo, hi, coef, emit):
    cx_ref, mid_ref, cy_ref = coef
    count, n = u_ref.shape[0], u_ref.shape[2]
    prev = u_ref[lo - 1] if lo > 0 else None
    cur = u_ref[lo]
    for x in range(lo, hi + 1):
        nxt = u_ref[x + 1] if x + 1 < count else None
        new = mid_ref[x : x + 1] * cur + (
            cy_ref[0:1] * pltpu.roll(cur, n - 1, 1) + cy_ref[1:2] * pltpu.roll(cur, 1, 1)
        )
        if nxt is not None:
            new = new + cx_ref[x : x + 1] * nxt
        if prev is not None:
            new = new + cx_ref[x - 1 : x] * prev
        emit(x, new)
        prev, cur = cur, nxt


def flat(shape):
    return pl.BlockSpec(shape, lambda i, k: (0,) * len(shape))


def smooth_kernel(_core, ctl_ref, cx_ref, mid_ref, cy_ref, out_ref, u_ref):
    cols = ctl_ref.shape[1]
    zero = jnp.zeros(u_ref.shape[1:], u_ref.dtype)
    for x in range(W):
        u_ref[x] = zero
        u_ref[W + cols + x] = zero
    for x in range(cols):
        u_ref[W + x] = ctl_ref[0, x]

    def keep(x, v):
        u_ref[x] = v

    def give(x, v):
        out_ref[0, x] = v.astype(out_ref.dtype)

    for step in range(1, STEPS + 1):
        emit = keep if step < STEPS else give
        sweep(u_ref, W - step, W + cols - 1 + step, (cx_ref, mid_ref, cy_ref), emit)


def smooth_call(core, control, coef, mine):
    m, cols, lev, cy = control.shape
    half = m // 2
    ext = cols + 2 * W

    def member(i, k):
        return ((k[0] if mine else 1 - k[0]) * half + i, 0, 0, 0)

    return pl.pallas_call(
        smooth_kernel,
        grid_spec=pltpu.PrefetchScalarGridSpec(
            num_scalar_prefetch=1,
            grid=(half,),
            in_specs=[pl.BlockSpec((1, cols, lev, cy), member)] + [flat(c.shape) for c in coef],
            out_specs=pl.BlockSpec((1, ext, lev, cy), lambda i, k: (i, 0, 0, 0)),
            scratch_shapes=[pltpu.VMEM((ext, lev, cy), jnp.float32)],
        ),
        out_shape=jax.ShapeDtypeStruct((half, ext, lev, cy), jnp.bfloat16),
        compiler_params=pltpu.CompilerParams(vmem_limit_bytes=32 * 2**20),
        cost_estimate=COST,
        name="smooth",
    )(core, control, *coef)


VMEM = pl.BlockSpec(memory_space=pltpu.VMEM)


def message_kernel(values_ref, cells_ref, counts_ref, out_ref):
    cap, lev, rows = values_ref.shape
    lanes = out_ref.shape[1]
    per = lanes // lev
    groups = cap // per
    counts = counts_ref[...]
    for k in range(groups):
        part = [jnp.where(k * per + a < counts, values_ref[k * per + a], jnp.float32(0.0)) for a in range(per)]
        out_ref[pl.ds(k, rows, stride=groups + 1), :] = jnp.concatenate(part, 0).T
    cells = jnp.concatenate([cells_ref[...].astype(jnp.float32), jnp.zeros((lanes - cap, rows), jnp.float32)], 0)
    out_ref[pl.ds(groups, rows, stride=groups + 1), :] = cells.T


def message_call(values, cells, counts, lanes):
    cap, lev, rows = values.shape
    return pl.pallas_call(
        message_kernel,
        out_shape=jax.ShapeDtypeStruct((rows * (cap * lev // lanes + 1), lanes), jnp.float32),
        in_specs=[VMEM] * 3,
        out_specs=VMEM,
        compiler_params=pltpu.CompilerParams(vmem_limit_bytes=16 * 2**20),
        cost_estimate=COST,
        name="message",
    )(values, cells, counts)


def scatter_kernel(cap, got_ref, out_ref):
    cols, lev, cy = out_ref.shape
    lanes = got_ref.shape[1]
    per = lanes // lev
    groups = cap // per
    senders = got_ref.shape[0] // (groups + 1)
    vals = jnp.concatenate([got_ref[pl.ds(k, senders, stride=groups + 1), :] for k in range(groups)], 0)
    cells = got_ref[pl.ds(groups, senders, stride=groups + 1), :]
    rows = vals.shape[0]
    vt = vals.T
    high = vt.astype(jnp.bfloat16)
    low = (vt - high.astype(jnp.float32)).astype(jnp.bfloat16)
    lane = lax.broadcasted_iota(jnp.int32, (rows, cy), 1)
    total = [jnp.zeros((2 * lev, cy), jnp.float32) for _ in range(cols)]
    for a in range(per):
        part = slice(a * lev, (a + 1) * lev)
        both = jnp.concatenate([high[part], low[part]], 0)
        at = jnp.concatenate([cells[:, k * per + a : k * per + a + 1] for k in range(groups)], 0)
        cell = jnp.broadcast_to(at, (rows, cy)).astype(jnp.int32) - lane
        for x in range(cols):
            hot = jnp.where(cell == x * cy, jnp.float32(1), jnp.float32(0)).astype(jnp.bfloat16)
            total[x] = total[x] + jnp.dot(both, hot, preferred_element_type=jnp.float32)
    for x in range(cols):
        out_ref[x] = total[x][:lev] + total[x][lev:]


def scatter_call(got, cap, cols, lev, cy):
    return pl.pallas_call(
        functools.partial(scatter_kernel, cap),
        out_shape=jax.ShapeDtypeStruct((cols, lev, cy), jnp.float32),
        in_specs=[VMEM],
        out_specs=VMEM,
        compiler_params=pltpu.CompilerParams(vmem_limit_bytes=32 * 2**20),
        cost_estimate=COST,
        name="scatter",
    )(got)


def order_kernel(j_ref, v_ref, vf_ref, vt_ref, rows_ref):
    lev = v_ref.shape[0] // 4

    def ordered(take):
        return jnp.concatenate([take(pl.ds(pl.multiple_of((j_ref[0] ^ b) * lev, lev), lev)) for b in range(4)], 0)

    rows_ref[...] = v_ref[...].astype(jnp.float32)
    rows_ref[...] = ordered(lambda at: rows_ref[at, :]).T
    turned = ordered(lambda at: rows_ref[at, :])[: 2 * lev]
    vt_ref[...] = turned.astype(vt_ref.dtype)
    vf_ref[...] = turned.T.astype(vf_ref.dtype)


def order_call(j, v):
    n = v.shape[0]
    return pl.pallas_call(
        order_kernel,
        out_shape=[jax.ShapeDtypeStruct((n, n // 2), v.dtype), jax.ShapeDtypeStruct((n // 2, n), v.dtype)],
        in_specs=[pl.BlockSpec(memory_space=pltpu.SMEM), VMEM],
        out_specs=[VMEM, VMEM],
        scratch_shapes=[pltpu.VMEM((n, n), jnp.float32)],
        cost_estimate=COST,
        name="order",
    )(j, v)


def forward_kernel(edges, *refs):
    e_refs, (s0_ref, s1_ref, vf_ref, inc_ref) = refs[:4], refs[4:]
    lev = inc_ref.shape[2]
    count = inc_ref.shape[1]

    @pl.when(pl.program_id(0) == 0)
    def _():
        inc_ref[...] = jnp.zeros(inc_ref.shape, inc_ref.dtype)

    def block(b, x):
        return halo(e_refs, b, x) if edges else e_refs[b][0, x]

    ext = s0_ref.shape[1]
    for x in range(0, count, 2):
        at = [(y if y < W else ext - 2 * W + y) if edges else y + W for y in (x, x + 1)]
        smooth = [jnp.concatenate([s0_ref[0, y], s1_ref[0, y]], 0) for y in at]
        local = jnp.dot(vf_ref[...], jnp.concatenate(smooth, 1), preferred_element_type=jnp.float32)
        width = local.shape[1] // 2
        for i, y in enumerate((x, x + 1)):
            for b in range(4):
                e = block(b, y).astype(jnp.float32)
                inc_ref[b, y] += e * local[b * lev : (b + 1) * lev, i * width : (i + 1) * width]


def halo(refs, b, x):
    return refs[x // W * 2 + b // 2][b % 2, 0, x % W]


def rows_of(array, start):
    return pl.BlockSpec((1,) + array.shape[1:], lambda i, *k: (start + i, 0, 0, 0))


def halo_of(array, start):
    return pl.BlockSpec((array.shape[0], 1) + array.shape[2:], lambda i, *k: (0, start + i, 0, 0, 0))


def forward_call(edges, e, s0, s1, vf):
    members, ext, lev, cy = s0.shape
    count = 2 * W if edges else ext - 2 * W
    spec_of = halo_of if edges else rows_of
    return pl.pallas_call(
        functools.partial(forward_kernel, edges),
        grid=(members,),
        in_specs=[spec_of(x, 0) for x in e] + [rows_of(s0, 0), rows_of(s1, 0), pl.BlockSpec(vf.shape, lambda i: (0, 0))],
        out_specs=pl.BlockSpec((4, count, lev, cy), lambda i: (0, 0, 0, 0)),
        out_shape=jax.ShapeDtypeStruct((4, count, lev, cy), jnp.float32),
        compiler_params=pltpu.CompilerParams(vmem_limit_bytes=32 * 2**20),
        cost_estimate=COST,
        name="edges" if edges else "inner",
    )(*e, s0, s1, vf)


def adjoint_kernel(_core, e0_ref, e1_ref, e2_ref, e3_ref, *refs):
    halos, refs = refs[:4], refs[4:]
    g_ref, vt_ref, cx_ref, mid_ref, cy_ref, ctl_ref = refs[:6]
    grad_ref, other_ref, u_ref = refs[-3:]
    cols, lev, _ = grad_ref.shape[1:]
    ext = cols + 2 * W
    def block(b, x):
        if W <= x < W + cols:
            return (e0_ref, e1_ref, e2_ref, e3_ref)[b][0, x - W]
        return halo(halos, b, x if x < W else x - cols)

    for x in range(0, ext, 2):
        weighted = []
        for y in (x, x + 1):
            weighted.append(
                jnp.concatenate([(block(b, y).astype(jnp.float32) * g_ref[b, y]).astype(jnp.bfloat16) for b in range(4)], 0)
            )
        back = jnp.dot(vt_ref[...], jnp.concatenate(weighted, 1), preferred_element_type=jnp.float32)
        width = back.shape[1] // 2
        for i, y in enumerate((x, x + 1)):
            u_ref[y] = back[:, i * width : (i + 1) * width]

    def keep(x, v):
        u_ref[x] = v

    def give(x, v):
        grad_ref[0, x - W] = ctl_ref[0, x - W] + v[:lev]
        other_ref[0, x - W] = v[lev:]

    for step in range(1, STEPS + 1):
        sweep(u_ref, step, ext - 1 - step, (cx_ref, mid_ref, cy_ref), keep if step < STEPS else give)


def adjoint_call(core, at, c, e, halos, g, vt, coef, control, grad):
    m, cols, lev, cy = control.shape
    half = m // 2
    ext = cols + 2 * W
    mine = pl.BlockSpec((1, cols, lev, cy), lambda i, k: (k[0] * half + at + i, 0, 0, 0))
    in_specs = [rows_of(x, at) for x in e] + [halo_of(x, at) for x in halos]
    in_specs += [flat(g.shape), flat(vt.shape)] + [flat(x.shape) for x in coef] + [mine]
    args = [*e, *halos, g, vt, *coef, control]
    aliases = {}
    if grad is not None:
        in_specs.append(pl.BlockSpec(memory_space=pl.ANY))
        args.append(grad)
        aliases = {len(args): 0}
    return pl.pallas_call(
        adjoint_kernel,
        grid_spec=pltpu.PrefetchScalarGridSpec(
            num_scalar_prefetch=1,
            grid=(c,),
            in_specs=in_specs,
            out_specs=[mine, pl.BlockSpec((1, cols, lev, cy), lambda i, k: (i, 0, 0, 0))],
            scratch_shapes=[pltpu.VMEM((ext, 2 * lev, cy), jnp.float32)],
        ),
        out_shape=[
            jax.ShapeDtypeStruct(control.shape, jnp.float32),
            jax.ShapeDtypeStruct((c, cols, lev, cy), jnp.float32),
        ],
        input_output_aliases=aliases,
        compiler_params=pltpu.CompilerParams(vmem_limit_bytes=40 * 2**20),
        cost_estimate=COST,
        name="adjoint",
    )(core, *args)


def finish_kernel(_core, r_ref, ctl_ref, _grad, out_ref):
    out_ref[...] = ctl_ref[...] + r_ref[...]


def finish_call(core, at, r, control, grad):
    c, cols, lev, cy = r.shape
    half = control.shape[0] // 2
    n = 2 if c % 2 == 0 and at % 2 == 0 and half % 2 == 0 else 1
    theirs = pl.BlockSpec((n, cols, lev, cy), lambda i, k: (((1 - k[0]) * half + at) // n + i, 0, 0, 0))
    return pl.pallas_call(
        finish_kernel,
        grid_spec=pltpu.PrefetchScalarGridSpec(
            num_scalar_prefetch=1,
            grid=(c // n,),
            in_specs=[pl.BlockSpec((n, cols, lev, cy), lambda i, k: (i, 0, 0, 0)), theirs, pl.BlockSpec(memory_space=pl.ANY)],
            out_specs=theirs,
        ),
        out_shape=jax.ShapeDtypeStruct(control.shape, jnp.float32),
        input_output_aliases={3: 0},
        compiler_params=pltpu.CompilerParams(vmem_limit_bytes=16 * 2**20),
        cost_estimate=COST,
        name="finish",
    )(core, r, control, grad)


def after(x, *first):
    return lax.optimization_barrier((x, first))[0]


def local(control, ensemble, coupling_x, coupling_y, vertical_loc, obs_cells, obs_counts, obs_values):
    m, lev, cols, cy = control.shape
    rows, cap = obs_cells.shape
    half = m // 2
    tile, j = lax.axis_index("tile"), lax.axis_index("lev")
    core, chip = j % 2, j // 2
    even = tile % 2 == 0
    low_edge, high_edge = tile % PLANE == 0, tile % PLANE == PLANE - 1
    facing = (low_edge & (chip == 0)) | (high_edge & (chip == 1))
    served = (low_edge & (chip == 1)) | (high_edge & (chip == 0))
    core_arg = core.astype(jnp.int32).reshape(1)
    control = jnp.transpose(control, (0, 2, 1, 3))
    ens = jnp.transpose(ensemble, (0, 2, 1, 3))

    def top(x):
        return x[:, cols - W :]

    def bottom(x):
        return x[:, :W]

    def payloads(pair):
        return (
            jnp.stack([jnp.where(even, top(x), bottom(x)) for x in pair]),
            jnp.stack([jnp.where(even, bottom(x), top(x)) for x in pair]),
        )

    cx_low, cx_high = beside_tile(even, coupling_x[cols - W :], coupling_x[:W])
    cxe = jnp.concatenate([cx_low, coupling_x, cx_high], 0)
    at_y = lax.broadcasted_iota(jnp.int32, (cy,), 0)
    north = jnp.where(at_y < cy - 1, coupling_y, jnp.float32(0.0))
    south = jnp.where(at_y > 0, jnp.roll(coupling_y, 1), jnp.float32(0.0))
    cxe_before = jnp.concatenate([cxe[:1], cxe[:-1]], 0)
    coef = (cxe, (1.0 - north - south) - (cxe + cxe_before), jnp.stack([north, south]))

    other = jnp.where(core == 0, ens[half:], ens[:half])
    mine = jnp.where(core == 0, ens[:half], ens[half:])
    beside = flip_core(other)
    far_mine, far_beside = flip_chip(mine), flip_chip(beside)
    own_send = payloads((mine, beside))
    own_first, own_second = swap_first(own_send[0]), swap_second_near(own_send[1])

    message = message_call(
        jnp.transpose(obs_values, (1, 2, 0)), after(obs_cells.T, own_send), obs_counts[None], 128
    )
    got = lax.all_to_all(message.reshape(rows, -1), "tile", split_axis=0, concat_axis=0, tiled=True)

    vf, vt = order_call(j.astype(jnp.int32).reshape(1), vertical_loc)

    smooth_send = smooth_call(core_arg, after(control, message, vf), coef, False)
    s1 = flip_core(smooth_send)
    s0 = smooth_call(core_arg, after(control, smooth_send), coef, True)

    relayed = relay(after(own_second, s0))
    got = after(got, s0, own_first, own_second, far_mine)
    g_own = scatter_call(got.reshape(message.shape), cap, cols, lev, cy)
    g_raw = g_own
    g_low, g_high = beside_tile(even, g_own[cols - W :], g_own[:W])
    g_own = jnp.concatenate([g_low, after(g_own, s1), g_high], 0)
    g_far = flip_chip(g_own)
    g_beside = flip_core(jnp.stack([g_own, g_far]))
    g = jnp.stack([g_own, g_beside[0], g_far, g_beside[1]])

    far_send = payloads((far_mine, after(far_beside, g_raw)))
    far_first = swap_first(far_send[0])
    far_second = swap_second_near(far_send[1])
    reached = reach(after(far_send[1], g_own))
    e = [mine, beside, far_mine, after(far_beside, far_send)]
    inner = forward_call(False, e, s0, s1, vf)

    own_outer = jnp.where(served, relayed, jnp.where(facing, far_second, own_second))
    far_outer = jnp.where(served, reached, jnp.where(facing, own_second, far_second))
    halos = [
        jnp.where(even, own_outer, own_first),
        jnp.where(even, far_outer, far_first),
        jnp.where(even, own_first, own_outer),
        jnp.where(even, far_first, far_outer),
    ]
    edges = forward_call(True, halos, s0, after(s1, inner), vf)
    def over_cores(part):
        return part[::2] + flip_core(part[1::2])

    def over_chips(pair):
        return pair[0] + flip_chip(pair[1])

    def adjoint(n, grad, *first):
        at, c = plan[n]
        return adjoint_call(core_arg, at, c, e, halos, after(g, first), vt, coef, control, grad)

    plan = chunks_of(half)
    inner = over_chips(over_cores(inner))
    grad, r = adjoint(0, None, edges)
    returned = [flip_core(r)]
    edges = over_chips(over_cores(edges))
    grad, r = adjoint(1, grad)
    returned.append(flip_core(r))
    edge_low, edge_high = beside_tile(even, edges[W:], edges[:W])
    grad = finish_call(core_arg, plan[0][0], returned[0], control, grad)
    grad, r = adjoint(2, grad, edges)
    returned.append(flip_core(r))
    for n in (1, 2):
        grad = finish_call(core_arg, plan[n][0], returned[n], control, grad)
    inc = jnp.concatenate([inner[:W] + edge_low, inner[W : cols - W], inner[cols - W :] + edge_high], 0)
    return jnp.transpose(inc, (1, 0, 2)), jnp.transpose(grad, (0, 2, 1, 3))


def solution(mesh):
    placed = (
        P(None, "lev", "tile", None),
        P(None, "lev", "tile", None),
        P("tile", None),
        P(),
        P(),
        P("tile", None),
        P("tile"),
        P("tile", None, "lev"),
    )
    return jax.shard_map(
        local,
        mesh=mesh,
        in_specs=placed,
        out_specs=(P("lev", "tile", None), P(None, "lev", "tile", None)),
        check_vma=False,
    )
```

```python
import functools

import jax
import jax.numpy as jnp
from jax import lax
from jax.experimental import pallas as pl
from jax.experimental.pallas import tpu as pltpu
from jax.sharding import PartitionSpec as P

STEPS = 4
W = STEPS
PLANE = 16
COST = pl.CostEstimate(flops=1, bytes_accessed=1, transcendentals=0)


def chunks_of(half):
    sizes = [half - 2 * (2 * half // 5), 2 * half // 5, 2 * half // 5]
    out, at = [], 0
    for s in sizes:
        if s:
            out.append((at, s))
            at += s
    return out


def permute(x, route):
    tiles, levs = lax.axis_size("tile"), lax.axis_size("lev")
    pairs = []
    for t in range(tiles):
        for j in range(levs):
            to = route(t, j)
            if to is not None:
                pairs.append((t * levs + j, (to[0] % tiles) * levs + to[1]))
    return lax.ppermute(x, ("tile", "lev"), pairs)


def flip_core(x):
    return permute(x, lambda t, j: (t, j ^ 1))


def flip_chip(x):
    return permute(x, lambda t, j: (t, j ^ 2))


def swap_first(x):
    return permute(x, lambda t, j: (t + 1 if t % 2 == 0 else t - 1, j))


def swap_second(x):
    return permute(x, lambda t, j: (t - 1 if t % 2 == 0 else t + 1, j))


def swap_second_near(x):
    def route(t, j):
        to = t - 1 if t % 2 == 0 else t + 1
        if t % PLANE == 0:
            return (to, j ^ 2) if j < 2 else None
        if t % PLANE == PLANE - 1:
            return (to, j ^ 2) if j >= 2 else None
        return (to, j)

    return permute(x, route)


def beside_tile(even, top, bottom):
    a = swap_first(jnp.where(even, top, bottom))
    b = swap_second(jnp.where(even, bottom, top))
    return jnp.where(even, b, a), jnp.where(even, a, b)


def relay(x):
    def route(t, j):
        if (t % PLANE == 0 and j < 2) or (t % PLANE == PLANE - 1 and j >= 2):
            return (t, j ^ 2)
        return None

    return permute(x, route)


def reach(x):
    def route(t, j):
        if t % PLANE == PLANE - 1 and j >= 2:
            return (t + 1, j)
        if t % PLANE == 0 and j < 2:
            return (t - 1, j)
        return None

    return permute(x, route)


def sweep(u_ref, lo, hi, coef, emit):
    cx_ref, mid_ref, cy_ref = coef
    count, n = u_ref.shape[0], u_ref.shape[2]
    prev = u_ref[lo - 1] if lo > 0 else None
    cur = u_ref[lo]
    for x in range(lo, hi + 1):
        nxt = u_ref[x + 1] if x + 1 < count else None
        new = mid_ref[x : x + 1] * cur + (
            cy_ref[0:1] * pltpu.roll(cur, n - 1, 1) + cy_ref[1:2] * pltpu.roll(cur, 1, 1)
        )
        if nxt is not None:
            new = new + cx_ref[x : x + 1] * nxt
        if prev is not None:
            new = new + cx_ref[x - 1 : x] * prev
        emit(x, new)
        prev, cur = cur, nxt


def flat(shape):
    return pl.BlockSpec(shape, lambda i, k: (0,) * len(shape))


def smooth_kernel(_core, ctl_ref, cx_ref, mid_ref, cy_ref, out_ref, u_ref):
    cols = ctl_ref.shape[1]
    zero = jnp.zeros(u_ref.shape[1:], u_ref.dtype)
    for x in range(W):
        u_ref[x] = zero
        u_ref[W + cols + x] = zero
    for x in range(cols):
        u_ref[W + x] = ctl_ref[0, x]

    def keep(x, v):
        u_ref[x] = v

    def give(x, v):
        out_ref[0, x] = v.astype(out_ref.dtype)

    for step in range(1, STEPS + 1):
        emit = keep if step < STEPS else give
        sweep(u_ref, W - step, W + cols - 1 + step, (cx_ref, mid_ref, cy_ref), emit)


def smooth_call(core, control, coef, mine):
    m, cols, lev, cy = control.shape
    half = m // 2
    ext = cols + 2 * W

    def member(i, k):
        return ((k[0] if mine else 1 - k[0]) * half + i, 0, 0, 0)

    return pl.pallas_call(
        smooth_kernel,
        grid_spec=pltpu.PrefetchScalarGridSpec(
            num_scalar_prefetch=1,
            grid=(half,),
            in_specs=[pl.BlockSpec((1, cols, lev, cy), member)] + [flat(c.shape) for c in coef],
            out_specs=pl.BlockSpec((1, ext, lev, cy), lambda i, k: (i, 0, 0, 0)),
            scratch_shapes=[pltpu.VMEM((ext, lev, cy), jnp.float32)],
        ),
        out_shape=jax.ShapeDtypeStruct((half, ext, lev, cy), jnp.bfloat16),
        compiler_params=pltpu.CompilerParams(vmem_limit_bytes=32 * 2**20),
        cost_estimate=COST,
        name="smooth",
    )(core, control, *coef)


VMEM = pl.BlockSpec(memory_space=pltpu.VMEM)


def message_kernel(values_ref, cells_ref, counts_ref, out_ref):
    cap, lev, rows = values_ref.shape
    lanes = out_ref.shape[1]
    per = lanes // lev
    groups = cap // per
    counts = counts_ref[...]
    for k in range(groups):
        part = [jnp.where(k * per + a < counts, values_ref[k * per + a], jnp.float32(0.0)) for a in range(per)]
        out_ref[pl.ds(k, rows, stride=groups + 1), :] = jnp.concatenate(part, 0).T
    cells = jnp.concatenate([cells_ref[...].astype(jnp.float32), jnp.zeros((lanes - cap, rows), jnp.float32)], 0)
    out_ref[pl.ds(groups, rows, stride=groups + 1), :] = cells.T


def message_call(values, cells, counts, lanes):
    cap, lev, rows = values.shape
    return pl.pallas_call(
        message_kernel,
        out_shape=jax.ShapeDtypeStruct((rows * (cap * lev // lanes + 1), lanes), jnp.float32),
        in_specs=[VMEM] * 3,
        out_specs=VMEM,
        compiler_params=pltpu.CompilerParams(vmem_limit_bytes=16 * 2**20),
        cost_estimate=COST,
        name="message",
    )(values, cells, counts)


def scatter_kernel(cap, got_ref, out_ref):
    cols, lev, cy = out_ref.shape
    lanes = got_ref.shape[1]
    per = lanes // lev
    groups = cap // per
    senders = got_ref.shape[0] // (groups + 1)
    vals = jnp.concatenate([got_ref[pl.ds(k, senders, stride=groups + 1), :] for k in range(groups)], 0)
    cells = got_ref[pl.ds(groups, senders, stride=groups + 1), :]
    rows = vals.shape[0]
    vt = vals.T
    high = vt.astype(jnp.bfloat16)
    low = (vt - high.astype(jnp.float32)).astype(jnp.bfloat16)
    lane = lax.broadcasted_iota(jnp.int32, (rows, cy), 1)
    total = [jnp.zeros((2 * lev, cy), jnp.float32) for _ in range(cols)]
    for a in range(per):
        part = slice(a * lev, (a + 1) * lev)
        both = jnp.concatenate([high[part], low[part]], 0)
        at = jnp.concatenate([cells[:, k * per + a : k * per + a + 1] for k in range(groups)], 0)
        cell = jnp.broadcast_to(at, (rows, cy)).astype(jnp.int32) - lane
        for x in range(cols):
            hot = jnp.where(cell == x * cy, jnp.float32(1), jnp.float32(0)).astype(jnp.bfloat16)
            total[x] = total[x] + jnp.dot(both, hot, preferred_element_type=jnp.float32)
    for x in range(cols):
        out_ref[x] = total[x][:lev] + total[x][lev:]


def scatter_call(got, cap, cols, lev, cy):
    return pl.pallas_call(
        functools.partial(scatter_kernel, cap),
        out_shape=jax.ShapeDtypeStruct((cols, lev, cy), jnp.float32),
        in_specs=[VMEM],
        out_specs=VMEM,
        compiler_params=pltpu.CompilerParams(vmem_limit_bytes=32 * 2**20),
        cost_estimate=COST,
        name="scatter",
    )(got)


def order_kernel(j_ref, v_ref, vf_ref, vt_ref, rows_ref):
    lev = v_ref.shape[0] // 4

    def ordered(take):
        return jnp.concatenate([take(pl.ds(pl.multiple_of((j_ref[0] ^ b) * lev, lev), lev)) for b in range(4)], 0)

    rows_ref[...] = v_ref[...].astype(jnp.float32)
    rows_ref[...] = ordered(lambda at: rows_ref[at, :]).T
    turned = ordered(lambda at: rows_ref[at, :])[: 2 * lev]
    vt_ref[...] = turned.astype(vt_ref.dtype)
    vf_ref[...] = turned.T.astype(vf_ref.dtype)


def order_call(j, v):
    n = v.shape[0]
    return pl.pallas_call(
        order_kernel,
        out_shape=[jax.ShapeDtypeStruct((n, n // 2), v.dtype), jax.ShapeDtypeStruct((n // 2, n), v.dtype)],
        in_specs=[pl.BlockSpec(memory_space=pltpu.SMEM), VMEM],
        out_specs=[VMEM, VMEM],
        scratch_shapes=[pltpu.VMEM((n, n), jnp.float32)],
        cost_estimate=COST,
        name="order",
    )(j, v)


def forward_kernel(edges, *refs):
    e_refs, s_refs, (vf_ref, inc_ref) = refs[:4], refs[4:-2], refs[-2:]
    lev = inc_ref.shape[2]
    count = inc_ref.shape[1]

    @pl.when(pl.program_id(0) == 0)
    def _():
        inc_ref[...] = jnp.zeros(inc_ref.shape, inc_ref.dtype)

    def block(b, x):
        return halo(e_refs, b, x) if edges else e_refs[b][0, x]

    def smooth_of(x):
        if edges:
            return jnp.concatenate([s_refs[i + x // W][0, x % W] for i in (0, 2)], 0)
        return jnp.concatenate([s[0, x + W] for s in s_refs], 0)

    for x in range(0, count, 2):
        smooth = [smooth_of(y) for y in (x, x + 1)]
        local = jnp.dot(vf_ref[...], jnp.concatenate(smooth, 1), preferred_element_type=jnp.float32)
        width = local.shape[1] // 2
        for i, y in enumerate((x, x + 1)):
            for b in range(4):
                e = block(b, y).astype(jnp.float32)
                inc_ref[b, y] += e * local[b * lev : (b + 1) * lev, i * width : (i + 1) * width]


def halo(refs, b, x):
    return refs[x // W * 2 + b // 2][b % 2, 0, x % W]


def rows_of(array, start):
    return pl.BlockSpec((1,) + array.shape[1:], lambda i, *k: (start + i, 0, 0, 0))


def halo_of(array, start):
    return pl.BlockSpec((array.shape[0], 1) + array.shape[2:], lambda i, *k: (0, start + i, 0, 0, 0))


def forward_call(edges, e, s0, s1, vf):
    members, ext, lev, cy = s0.shape
    count = 2 * W if edges else ext - 2 * W
    if edges:
        ends = [pl.BlockSpec((1, W, lev, cy), lambda i, n=n: (i, n, 0, 0)) for n in (0, ext // W - 1)]
        specs, s = [halo_of(x, 0) for x in e] + ends + ends, [s0, s0, s1, s1]
    else:
        specs, s = [rows_of(x, 0) for x in (*e, s0, s1)], [s0, s1]
    return pl.pallas_call(
        functools.partial(forward_kernel, edges),
        grid=(members,),
        in_specs=specs + [pl.BlockSpec(vf.shape, lambda i: (0, 0))],
        out_specs=pl.BlockSpec((4, count, lev, cy), lambda i: (0, 0, 0, 0)),
        out_shape=jax.ShapeDtypeStruct((4, count, lev, cy), jnp.float32),
        compiler_params=pltpu.CompilerParams(vmem_limit_bytes=32 * 2**20),
        cost_estimate=COST,
        name="edges" if edges else "inner",
    )(*e, *s, vf)


def adjoint_kernel(_core, e0_ref, e1_ref, e2_ref, e3_ref, *refs):
    halos, refs = refs[:4], refs[4:]
    g_ref, vt_ref, cx_ref, mid_ref, cy_ref, ctl_ref = refs[:6]
    grad_ref, other_ref, u_ref = refs[-3:]
    cols, lev, _ = grad_ref.shape[1:]
    ext = cols + 2 * W
    def block(b, x):
        if W <= x < W + cols:
            return (e0_ref, e1_ref, e2_ref, e3_ref)[b][0, x - W]
        return halo(halos, b, x if x < W else x - cols)

    for x in range(0, ext, 2):
        weighted = []
        for y in (x, x + 1):
            weighted.append(
                jnp.concatenate([(block(b, y).astype(jnp.float32) * g_ref[b, y]).astype(jnp.bfloat16) for b in range(4)], 0)
            )
        back = jnp.dot(vt_ref[...], jnp.concatenate(weighted, 1), preferred_element_type=jnp.float32)
        width = back.shape[1] // 2
        for i, y in enumerate((x, x + 1)):
            u_ref[y] = back[:, i * width : (i + 1) * width]

    def keep(x, v):
        u_ref[x] = v

    def give(x, v):
        grad_ref[0, x - W] = ctl_ref[0, x - W] + v[:lev]
        other_ref[0, x - W] = v[lev:]

    for step in range(1, STEPS + 1):
        sweep(u_ref, step, ext - 1 - step, (cx_ref, mid_ref, cy_ref), keep if step < STEPS else give)


def adjoint_call(core, at, c, e, halos, g, vt, coef, control, grad):
    m, cols, lev, cy = control.shape
    half = m // 2
    ext = cols + 2 * W
    mine = pl.BlockSpec((1, cols, lev, cy), lambda i, k: (k[0] * half + at + i, 0, 0, 0))
    in_specs = [rows_of(x, at) for x in e] + [halo_of(x, at) for x in halos]
    in_specs += [flat(g.shape), flat(vt.shape)] + [flat(x.shape) for x in coef] + [mine]
    args = [*e, *halos, g, vt, *coef, control]
    aliases = {}
    if grad is not None:
        in_specs.append(pl.BlockSpec(memory_space=pl.ANY))
        args.append(grad)
        aliases = {len(args): 0}
    return pl.pallas_call(
        adjoint_kernel,
        grid_spec=pltpu.PrefetchScalarGridSpec(
            num_scalar_prefetch=1,
            grid=(c,),
            in_specs=in_specs,
            out_specs=[mine, pl.BlockSpec((1, cols, lev, cy), lambda i, k: (i, 0, 0, 0))],
            scratch_shapes=[pltpu.VMEM((ext, 2 * lev, cy), jnp.float32)],
        ),
        out_shape=[
            jax.ShapeDtypeStruct(control.shape, jnp.float32),
            jax.ShapeDtypeStruct((c, cols, lev, cy), jnp.float32),
        ],
        input_output_aliases=aliases,
        compiler_params=pltpu.CompilerParams(vmem_limit_bytes=40 * 2**20),
        cost_estimate=COST,
        name="adjoint",
    )(core, *args)


def finish_kernel(_core, r_ref, ctl_ref, _grad, out_ref):
    out_ref[...] = ctl_ref[...] + r_ref[...]


def finish_call(core, at, r, control, grad):
    c, cols, lev, cy = r.shape
    half = control.shape[0] // 2
    n = 2 if c % 2 == 0 and at % 2 == 0 and half % 2 == 0 else 1
    theirs = pl.BlockSpec((n, cols, lev, cy), lambda i, k: (((1 - k[0]) * half + at) // n + i, 0, 0, 0))
    return pl.pallas_call(
        finish_kernel,
        grid_spec=pltpu.PrefetchScalarGridSpec(
            num_scalar_prefetch=1,
            grid=(c // n,),
            in_specs=[pl.BlockSpec((n, cols, lev, cy), lambda i, k: (i, 0, 0, 0)), theirs, pl.BlockSpec(memory_space=pl.ANY)],
            out_specs=theirs,
        ),
        out_shape=jax.ShapeDtypeStruct(control.shape, jnp.float32),
        input_output_aliases={3: 0},
        compiler_params=pltpu.CompilerParams(vmem_limit_bytes=16 * 2**20),
        cost_estimate=COST,
        name="finish",
    )(core, r, control, grad)


def after(x, *first):
    return lax.optimization_barrier((x, first))[0]


def local(control, ensemble, coupling_x, coupling_y, vertical_loc, obs_cells, obs_counts, obs_values):
    m, lev, cols, cy = control.shape
    rows, cap = obs_cells.shape
    half = m // 2
    tile, j = lax.axis_index("tile"), lax.axis_index("lev")
    core, chip = j % 2, j // 2
    even = tile % 2 == 0
    low_edge, high_edge = tile % PLANE == 0, tile % PLANE == PLANE - 1
    facing = (low_edge & (chip == 0)) | (high_edge & (chip == 1))
    served = (low_edge & (chip == 1)) | (high_edge & (chip == 0))
    core_arg = core.astype(jnp.int32).reshape(1)
    control = jnp.transpose(control, (0, 2, 1, 3))
    ens = jnp.transpose(ensemble, (0, 2, 1, 3))

    def top(x):
        return x[:, cols - W :]

    def bottom(x):
        return x[:, :W]

    def payloads(pair):
        return (
            jnp.stack([jnp.where(even, top(x), bottom(x)) for x in pair]),
            jnp.stack([jnp.where(even, bottom(x), top(x)) for x in pair]),
        )

    cx_low, cx_high = beside_tile(even, coupling_x[cols - W :], coupling_x[:W])
    cxe = jnp.concatenate([cx_low, coupling_x, cx_high], 0)
    at_y = lax.broadcasted_iota(jnp.int32, (cy,), 0)
    north = jnp.where(at_y < cy - 1, coupling_y, jnp.float32(0.0))
    south = jnp.where(at_y > 0, jnp.roll(coupling_y, 1), jnp.float32(0.0))
    cxe_before = jnp.concatenate([cxe[:1], cxe[:-1]], 0)
    coef = (cxe, (1.0 - north - south) - (cxe + cxe_before), jnp.stack([north, south]))

    other = jnp.where(core == 0, ens[half:], ens[:half])
    mine = jnp.where(core == 0, ens[:half], ens[half:])
    beside = flip_core(other)
    far_mine, far_beside = flip_chip(mine), flip_chip(beside)
    own_send = payloads((mine, beside))
    own_first, own_second = swap_first(own_send[0]), swap_second_near(own_send[1])

    message = message_call(
        jnp.transpose(obs_values, (1, 2, 0)), after(obs_cells.T, own_send), obs_counts[None], 128
    )
    got = lax.all_to_all(message.reshape(rows, -1), "tile", split_axis=0, concat_axis=0, tiled=True)

    vf, vt = order_call(j.astype(jnp.int32).reshape(1), vertical_loc)

    smooth_send = smooth_call(core_arg, after(control, message, vf), coef, False)
    s1 = flip_core(smooth_send)
    s0 = smooth_call(core_arg, after(control, smooth_send), coef, True)

    relayed = relay(after(own_second, s0))
    got = after(got, s0, own_first, own_second, far_mine)
    g_own = scatter_call(got.reshape(message.shape), cap, cols, lev, cy)
    g_low, g_high = beside_tile(even, g_own[cols - W :], g_own[:W])
    g_own = jnp.concatenate([g_low, after(g_own, s1), g_high], 0)
    g_far = flip_chip(g_own)
    g_beside = flip_core(jnp.stack([g_own, g_far]))
    g = jnp.stack([g_own, g_beside[0], g_far, g_beside[1]])

    far_send = payloads((far_mine, after(far_beside, g_own)))
    far_first = swap_first(far_send[0])
    far_second = swap_second_near(far_send[1])
    reached = reach(far_send[1])
    e = [mine, beside, far_mine, after(far_beside, far_send)]
    inner = forward_call(False, e, s0, s1, vf)

    own_outer = jnp.where(served, relayed, jnp.where(facing, far_second, own_second))
    far_outer = jnp.where(served, reached, jnp.where(facing, own_second, far_second))
    halos = [
        jnp.where(even, own_outer, own_first),
        jnp.where(even, far_outer, far_first),
        jnp.where(even, own_first, own_outer),
        jnp.where(even, far_first, far_outer),
    ]
    edges = forward_call(True, halos, s0, after(s1, inner), vf)
    def over_cores(part):
        return part[::2] + flip_core(part[1::2])

    def adjoint(n, grad, *first):
        at, c = plan[n]
        return adjoint_call(core_arg, at, c, e, halos, after(g, first), vt, coef, control, grad)

    plan = chunks_of(half)
    inner = over_cores(inner)
    grad, r = adjoint(0, None, edges)
    returned = [flip_core(r)]
    edges = over_cores(edges)
    edge_low, edge_high = beside_tile(even, edges[:, W:], edges[:, :W])
    grad, r = adjoint(1, grad, edges)
    returned.append(flip_core(r))
    inc = jnp.concatenate([inner[:, :W] + edge_low, inner[:, W : cols - W], inner[:, cols - W :] + edge_high], 1)
    inc = inc[0] + flip_chip(inc[1])
    grad = finish_call(core_arg, plan[0][0], returned[0], control, grad)
    grad, r = adjoint(2, grad)
    returned.append(flip_core(r))
    for n in (1, 2):
        grad = finish_call(core_arg, plan[n][0], returned[n], control, grad)
    return jnp.transpose(inc, (1, 0, 2)), jnp.transpose(grad, (0, 2, 1, 3))


def solution(mesh):
    placed = (
        P(None, "lev", "tile", None),
        P(None, "lev", "tile", None),
        P("tile", None),
        P(),
        P(),
        P("tile", None),
        P("tile"),
        P("tile", None, "lev"),
    )
    return jax.shard_map(
        local,
        mesh=mesh,
        in_specs=placed,
        out_specs=(P("lev", "tile", None), P(None, "lev", "tile", None)),
        check_vma=False,
    )
```

```python
import functools

import jax
import jax.numpy as jnp
from jax import lax
from jax.experimental import pallas as pl
from jax.experimental.pallas import tpu as pltpu
from jax.sharding import PartitionSpec as P

STEPS = 4
W = STEPS
PLANE = 16
COST = pl.CostEstimate(flops=1, bytes_accessed=1, transcendentals=0)


def chunks_of(half):
    sizes = [half - 2 * half // 5, 2 * half // 5]
    out, at = [], 0
    for s in sizes:
        if s:
            out.append((at, s))
            at += s
    return out


def permute(x, route):
    tiles, levs = lax.axis_size("tile"), lax.axis_size("lev")
    pairs = []
    for t in range(tiles):
        for j in range(levs):
            to = route(t, j)
            if to is not None:
                pairs.append((t * levs + j, (to[0] % tiles) * levs + to[1]))
    return lax.ppermute(x, ("tile", "lev"), pairs)


def flip_core(x):
    return permute(x, lambda t, j: (t, j ^ 1))


def flip_chip(x):
    return permute(x, lambda t, j: (t, j ^ 2))


def swap_first(x):
    return permute(x, lambda t, j: (t + 1 if t % 2 == 0 else t - 1, j))


def swap_second(x):
    return permute(x, lambda t, j: (t - 1 if t % 2 == 0 else t + 1, j))


def swap_second_near(x):
    def route(t, j):
        to = t - 1 if t % 2 == 0 else t + 1
        if t % PLANE == 0:
            return (to, j ^ 2) if j < 2 else None
        if t % PLANE == PLANE - 1:
            return (to, j ^ 2) if j >= 2 else None
        return (to, j)

    return permute(x, route)


def beside_tile(even, top, bottom):
    a = swap_first(jnp.where(even, top, bottom))
    b = swap_second(jnp.where(even, bottom, top))
    return jnp.where(even, b, a), jnp.where(even, a, b)


def relay(x):
    def route(t, j):
        if (t % PLANE == 0 and j < 2) or (t % PLANE == PLANE - 1 and j >= 2):
            return (t, j ^ 2)
        return None

    return permute(x, route)


def reach(x):
    def route(t, j):
        if t % PLANE == PLANE - 1 and j >= 2:
            return (t + 1, j)
        if t % PLANE == 0 and j < 2:
            return (t - 1, j)
        return None

    return permute(x, route)


def sweep(u_ref, lo, hi, coef, emit):
    cx_ref, mid_ref, cy_ref = coef
    count, n = u_ref.shape[0], u_ref.shape[2]
    prev = u_ref[lo - 1] if lo > 0 else None
    cur = u_ref[lo]
    for x in range(lo, hi + 1):
        nxt = u_ref[x + 1] if x + 1 < count else None
        new = mid_ref[x : x + 1] * cur + (
            cy_ref[0:1] * pltpu.roll(cur, n - 1, 1) + cy_ref[1:2] * pltpu.roll(cur, 1, 1)
        )
        if nxt is not None:
            new = new + cx_ref[x : x + 1] * nxt
        if prev is not None:
            new = new + cx_ref[x - 1 : x] * prev
        emit(x, new)
        prev, cur = cur, nxt


def flat(shape):
    return pl.BlockSpec(shape, lambda i, k: (0,) * len(shape))


def smooth_kernel(_core, ctl_ref, cx_ref, mid_ref, cy_ref, out_ref, u_ref):
    cols = ctl_ref.shape[1]
    zero = jnp.zeros(u_ref.shape[1:], u_ref.dtype)
    for x in range(W):
        u_ref[x] = zero
        u_ref[W + cols + x] = zero
    for x in range(cols):
        u_ref[W + x] = ctl_ref[0, x]

    def keep(x, v):
        u_ref[x] = v

    def give(x, v):
        out_ref[0, x] = v.astype(out_ref.dtype)

    for step in range(1, STEPS + 1):
        emit = keep if step < STEPS else give
        sweep(u_ref, W - step, W + cols - 1 + step, (cx_ref, mid_ref, cy_ref), emit)


def smooth_call(core, control, coef, mine):
    m, cols, lev, cy = control.shape
    half = m // 2
    ext = cols + 2 * W

    def member(i, k):
        return ((k[0] if mine else 1 - k[0]) * half + i, 0, 0, 0)

    return pl.pallas_call(
        smooth_kernel,
        grid_spec=pltpu.PrefetchScalarGridSpec(
            num_scalar_prefetch=1,
            grid=(half,),
            in_specs=[pl.BlockSpec((1, cols, lev, cy), member)] + [flat(c.shape) for c in coef],
            out_specs=pl.BlockSpec((1, ext, lev, cy), lambda i, k: (i, 0, 0, 0)),
            scratch_shapes=[pltpu.VMEM((ext, lev, cy), jnp.float32)],
        ),
        out_shape=jax.ShapeDtypeStruct((half, ext, lev, cy), jnp.bfloat16),
        compiler_params=pltpu.CompilerParams(vmem_limit_bytes=32 * 2**20),
        cost_estimate=COST,
        name="smooth",
    )(core, control, *coef)


VMEM = pl.BlockSpec(memory_space=pltpu.VMEM)


def message_kernel(values_ref, cells_ref, counts_ref, out_ref):
    cap, lev, rows = values_ref.shape
    lanes = out_ref.shape[1]
    per = lanes // lev
    groups = cap // per
    counts = counts_ref[...]
    for k in range(groups):
        part = [jnp.where(k * per + a < counts, values_ref[k * per + a], jnp.float32(0.0)) for a in range(per)]
        out_ref[pl.ds(k, rows, stride=groups + 1), :] = jnp.concatenate(part, 0).T
    cells = jnp.concatenate([cells_ref[...].astype(jnp.float32), jnp.zeros((lanes - cap, rows), jnp.float32)], 0)
    out_ref[pl.ds(groups, rows, stride=groups + 1), :] = cells.T


def message_call(values, cells, counts, lanes):
    cap, lev, rows = values.shape
    return pl.pallas_call(
        message_kernel,
        out_shape=jax.ShapeDtypeStruct((rows * (cap * lev // lanes + 1), lanes), jnp.float32),
        in_specs=[VMEM] * 3,
        out_specs=VMEM,
        compiler_params=pltpu.CompilerParams(vmem_limit_bytes=16 * 2**20),
        cost_estimate=COST,
        name="message",
    )(values, cells, counts)


def scatter_kernel(cap, got_ref, out_ref):
    cols, lev, cy = out_ref.shape
    lanes = got_ref.shape[1]
    per = lanes // lev
    groups = cap // per
    senders = got_ref.shape[0] // (groups + 1)
    vals = jnp.concatenate([got_ref[pl.ds(k, senders, stride=groups + 1), :] for k in range(groups)], 0)
    cells = got_ref[pl.ds(groups, senders, stride=groups + 1), :]
    rows = vals.shape[0]
    vt = vals.T
    high = vt.astype(jnp.bfloat16)
    low = (vt - high.astype(jnp.float32)).astype(jnp.bfloat16)
    lane = lax.broadcasted_iota(jnp.int32, (rows, cy), 1)
    total = [jnp.zeros((2 * lev, cy), jnp.float32) for _ in range(cols)]
    for a in range(per):
        part = slice(a * lev, (a + 1) * lev)
        both = jnp.concatenate([high[part], low[part]], 0)
        at = jnp.concatenate([cells[:, k * per + a : k * per + a + 1] for k in range(groups)], 0)
        cell = jnp.broadcast_to(at, (rows, cy)).astype(jnp.int32) - lane
        for x in range(cols):
            hot = jnp.where(cell == x * cy, jnp.float32(1), jnp.float32(0)).astype(jnp.bfloat16)
            total[x] = total[x] + jnp.dot(both, hot, preferred_element_type=jnp.float32)
    for x in range(cols):
        out_ref[x] = total[x][:lev] + total[x][lev:]


def scatter_call(got, cap, cols, lev, cy):
    return pl.pallas_call(
        functools.partial(scatter_kernel, cap),
        out_shape=jax.ShapeDtypeStruct((cols, lev, cy), jnp.float32),
        in_specs=[VMEM],
        out_specs=VMEM,
        compiler_params=pltpu.CompilerParams(vmem_limit_bytes=32 * 2**20),
        cost_estimate=COST,
        name="scatter",
    )(got)


def order_kernel(j_ref, v_ref, vf_ref, vt_ref, rows_ref):
    lev = v_ref.shape[0] // 4

    def ordered(take):
        return jnp.concatenate([take(pl.ds(pl.multiple_of((j_ref[0] ^ b) * lev, lev), lev)) for b in range(4)], 0)

    rows_ref[...] = v_ref[...].astype(jnp.float32)
    rows_ref[...] = ordered(lambda at: rows_ref[at, :]).T
    turned = ordered(lambda at: rows_ref[at, :])[: 2 * lev]
    vt_ref[...] = turned.astype(vt_ref.dtype)
    vf_ref[...] = turned.T.astype(vf_ref.dtype)


def order_call(j, v):
    n = v.shape[0]
    return pl.pallas_call(
        order_kernel,
        out_shape=[jax.ShapeDtypeStruct((n, n // 2), v.dtype), jax.ShapeDtypeStruct((n // 2, n), v.dtype)],
        in_specs=[pl.BlockSpec(memory_space=pltpu.SMEM), VMEM],
        out_specs=[VMEM, VMEM],
        scratch_shapes=[pltpu.VMEM((n, n), jnp.float32)],
        cost_estimate=COST,
        name="order",
    )(j, v)


def forward_kernel(edges, *refs):
    e_refs, s_refs, (vf_ref, inc_ref) = refs[:4], refs[4:-2], refs[-2:]
    lev = inc_ref.shape[2]
    count = inc_ref.shape[1]

    @pl.when(pl.program_id(0) == 0)
    def _():
        inc_ref[...] = jnp.zeros(inc_ref.shape, inc_ref.dtype)

    def block(b, x):
        return halo(e_refs, b, x) if edges else e_refs[b][0, x]

    def smooth_of(x):
        if edges:
            return jnp.concatenate([s_refs[i + x // W][0, x % W] for i in (0, 2)], 0)
        return jnp.concatenate([s[0, x + W] for s in s_refs], 0)

    for x in range(0, count, 2):
        smooth = [smooth_of(y) for y in (x, x + 1)]
        local = jnp.dot(vf_ref[...], jnp.concatenate(smooth, 1), preferred_element_type=jnp.float32)
        width = local.shape[1] // 2
        for i, y in enumerate((x, x + 1)):
            for b in range(4):
                e = block(b, y).astype(jnp.float32)
                inc_ref[b, y] += e * local[b * lev : (b + 1) * lev, i * width : (i + 1) * width]


def halo(refs, b, x):
    return refs[x // W * 2 + b // 2][b % 2, 0, x % W]


def rows_of(array, start):
    return pl.BlockSpec((1,) + array.shape[1:], lambda i, *k: (start + i, 0, 0, 0))


def halo_of(array, start):
    return pl.BlockSpec((array.shape[0], 1) + array.shape[2:], lambda i, *k: (0, start + i, 0, 0, 0))


def forward_call(edges, e, s0, s1, vf):
    members, ext, lev, cy = s0.shape
    count = 2 * W if edges else ext - 2 * W
    if edges:
        ends = [pl.BlockSpec((1, W, lev, cy), lambda i, n=n: (i, n, 0, 0)) for n in (0, ext // W - 1)]
        specs, s = [halo_of(x, 0) for x in e] + ends + ends, [s0, s0, s1, s1]
    else:
        specs, s = [rows_of(x, 0) for x in (*e, s0, s1)], [s0, s1]
    return pl.pallas_call(
        functools.partial(forward_kernel, edges),
        grid=(members,),
        in_specs=specs + [pl.BlockSpec(vf.shape, lambda i: (0, 0))],
        out_specs=pl.BlockSpec((4, count, lev, cy), lambda i: (0, 0, 0, 0)),
        out_shape=jax.ShapeDtypeStruct((4, count, lev, cy), jnp.float32),
        compiler_params=pltpu.CompilerParams(vmem_limit_bytes=32 * 2**20),
        cost_estimate=COST,
        name="edges" if edges else "inner",
    )(*e, *s, vf)


def adjoint_kernel(_core, e0_ref, e1_ref, e2_ref, e3_ref, *refs):
    halos, refs = refs[:4], refs[4:]
    g_ref, vt_ref, cx_ref, mid_ref, cy_ref, ctl_ref = refs[:6]
    grad_ref, other_ref, u_ref = refs[-3:]
    cols, lev, _ = grad_ref.shape[1:]
    ext = cols + 2 * W
    def block(b, x):
        if W <= x < W + cols:
            return (e0_ref, e1_ref, e2_ref, e3_ref)[b][0, x - W]
        return halo(halos, b, x if x < W else x - cols)

    for x in range(0, ext, 2):
        weighted = []
        for y in (x, x + 1):
            weighted.append(
                jnp.concatenate([(block(b, y).astype(jnp.float32) * g_ref[b, y]).astype(jnp.bfloat16) for b in range(4)], 0)
            )
        back = jnp.dot(vt_ref[...], jnp.concatenate(weighted, 1), preferred_element_type=jnp.float32)
        width = back.shape[1] // 2
        for i, y in enumerate((x, x + 1)):
            u_ref[y] = back[:, i * width : (i + 1) * width]

    def keep(x, v):
        u_ref[x] = v

    def give(x, v):
        grad_ref[0, x - W] = ctl_ref[0, x - W] + v[:lev]
        other_ref[0, x - W] = v[lev:]

    for step in range(1, STEPS + 1):
        sweep(u_ref, step, ext - 1 - step, (cx_ref, mid_ref, cy_ref), keep if step < STEPS else give)


def adjoint_call(core, at, c, e, halos, g, vt, coef, control, grad):
    m, cols, lev, cy = control.shape
    half = m // 2
    ext = cols + 2 * W
    mine = pl.BlockSpec((1, cols, lev, cy), lambda i, k: (k[0] * half + at + i, 0, 0, 0))
    in_specs = [rows_of(x, at) for x in e] + [halo_of(x, at) for x in halos]
    in_specs += [flat(g.shape), flat(vt.shape)] + [flat(x.shape) for x in coef] + [mine]
    args = [*e, *halos, g, vt, *coef, control]
    aliases = {}
    if grad is not None:
        in_specs.append(pl.BlockSpec(memory_space=pl.ANY))
        args.append(grad)
        aliases = {len(args): 0}
    return pl.pallas_call(
        adjoint_kernel,
        grid_spec=pltpu.PrefetchScalarGridSpec(
            num_scalar_prefetch=1,
            grid=(c,),
            in_specs=in_specs,
            out_specs=[mine, pl.BlockSpec((1, cols, lev, cy), lambda i, k: (i, 0, 0, 0))],
            scratch_shapes=[pltpu.VMEM((ext, 2 * lev, cy), jnp.float32)],
        ),
        out_shape=[
            jax.ShapeDtypeStruct(control.shape, jnp.float32),
            jax.ShapeDtypeStruct((c, cols, lev, cy), jnp.float32),
        ],
        input_output_aliases=aliases,
        compiler_params=pltpu.CompilerParams(vmem_limit_bytes=40 * 2**20),
        cost_estimate=COST,
        name="adjoint",
    )(core, *args)


def finish_kernel(_core, r_ref, ctl_ref, _grad, out_ref):
    out_ref[...] = ctl_ref[...] + r_ref[...]


def finish_call(core, at, r, control, grad):
    c, cols, lev, cy = r.shape
    half = control.shape[0] // 2
    n = 2 if c % 2 == 0 and at % 2 == 0 and half % 2 == 0 else 1
    theirs = pl.BlockSpec((n, cols, lev, cy), lambda i, k: (((1 - k[0]) * half + at) // n + i, 0, 0, 0))
    return pl.pallas_call(
        finish_kernel,
        grid_spec=pltpu.PrefetchScalarGridSpec(
            num_scalar_prefetch=1,
            grid=(c // n,),
            in_specs=[pl.BlockSpec((n, cols, lev, cy), lambda i, k: (i, 0, 0, 0)), theirs, pl.BlockSpec(memory_space=pl.ANY)],
            out_specs=theirs,
        ),
        out_shape=jax.ShapeDtypeStruct(control.shape, jnp.float32),
        input_output_aliases={3: 0},
        compiler_params=pltpu.CompilerParams(vmem_limit_bytes=16 * 2**20),
        cost_estimate=COST,
        name="finish",
    )(core, r, control, grad)


def after(x, *first):
    return lax.optimization_barrier((x, first))[0]


def local(control, ensemble, coupling_x, coupling_y, vertical_loc, obs_cells, obs_counts, obs_values):
    m, lev, cols, cy = control.shape
    rows, cap = obs_cells.shape
    half = m // 2
    tile, j = lax.axis_index("tile"), lax.axis_index("lev")
    core, chip = j % 2, j // 2
    even = tile % 2 == 0
    low_edge, high_edge = tile % PLANE == 0, tile % PLANE == PLANE - 1
    facing = (low_edge & (chip == 0)) | (high_edge & (chip == 1))
    served = (low_edge & (chip == 1)) | (high_edge & (chip == 0))
    core_arg = core.astype(jnp.int32).reshape(1)
    control = jnp.transpose(control, (0, 2, 1, 3))
    ens = jnp.transpose(ensemble, (0, 2, 1, 3))

    def top(x):
        return x[:, cols - W :]

    def bottom(x):
        return x[:, :W]

    def payloads(pair):
        return (
            jnp.stack([jnp.where(even, top(x), bottom(x)) for x in pair]),
            jnp.stack([jnp.where(even, bottom(x), top(x)) for x in pair]),
        )

    cx_low, cx_high = beside_tile(even, coupling_x[cols - W :], coupling_x[:W])
    cxe = jnp.concatenate([cx_low, coupling_x, cx_high], 0)
    at_y = lax.broadcasted_iota(jnp.int32, (cy,), 0)
    north = jnp.where(at_y < cy - 1, coupling_y, jnp.float32(0.0))
    south = jnp.where(at_y > 0, jnp.roll(coupling_y, 1), jnp.float32(0.0))
    cxe_before = jnp.concatenate([cxe[:1], cxe[:-1]], 0)
    coef = (cxe, (1.0 - north - south) - (cxe + cxe_before), jnp.stack([north, south]))

    other = jnp.where(core == 0, ens[half:], ens[:half])
    mine = jnp.where(core == 0, ens[:half], ens[half:])
    beside = flip_core(other)
    far_mine, far_beside = flip_chip(mine), flip_chip(beside)
    own_send = payloads((mine, beside))
    own_first, own_second = swap_first(own_send[0]), swap_second_near(own_send[1])

    message = message_call(
        jnp.transpose(obs_values, (1, 2, 0)), after(obs_cells.T, own_send), obs_counts[None], 128
    )
    got = lax.all_to_all(message.reshape(rows, -1), "tile", split_axis=0, concat_axis=0, tiled=True)

    vf, vt = order_call(j.astype(jnp.int32).reshape(1), vertical_loc)

    smooth_send = smooth_call(core_arg, after(control, message, vf), coef, False)
    s1 = flip_core(smooth_send)
    s0 = smooth_call(core_arg, after(control, smooth_send), coef, True)

    relayed = relay(after(own_second, s0))
    got = after(got, s0, own_first, own_second, far_mine)
    g_own = scatter_call(got.reshape(message.shape), cap, cols, lev, cy)
    g_low, g_high = beside_tile(even, g_own[cols - W :], g_own[:W])
    g_own = jnp.concatenate([g_low, after(g_own, s1), g_high], 0)
    g_far = flip_chip(g_own)
    g_beside = flip_core(jnp.stack([g_own, g_far]))
    g = jnp.stack([g_own, g_beside[0], g_far, g_beside[1]])

    far_send = payloads((far_mine, after(far_beside, g_own)))
    far_first = swap_first(far_send[0])
    far_second = swap_second_near(far_send[1])
    reached = reach(far_send[1])
    e = [mine, beside, far_mine, after(far_beside, far_send)]
    inner = forward_call(False, e, s0, s1, vf)

    own_outer = jnp.where(served, relayed, jnp.where(facing, far_second, own_second))
    far_outer = jnp.where(served, reached, jnp.where(facing, own_second, far_second))
    halos = [
        jnp.where(even, own_outer, own_first),
        jnp.where(even, far_outer, far_first),
        jnp.where(even, own_first, own_outer),
        jnp.where(even, far_first, far_outer),
    ]
    edges = forward_call(True, halos, s0, after(s1, inner), vf)
    def over_cores(part):
        return part[::2] + flip_core(part[1::2])

    def adjoint(n, grad, *first):
        at, c = plan[n]
        return adjoint_call(core_arg, at, c, e, halos, after(g, first), vt, coef, control, grad)

    plan = chunks_of(half)
    inner = over_cores(inner)
    grad, r = adjoint(0, None, edges)
    returned = [flip_core(r)]
    edges = over_cores(edges)
    edge_low, edge_high = beside_tile(even, edges[:, W:], edges[:, :W])
    grad, r = adjoint(1, grad, edges)
    returned.append(flip_core(r))
    inc = jnp.concatenate([inner[:, :W] + edge_low, inner[:, W : cols - W], inner[:, cols - W :] + edge_high], 1)
    inc = inc[0] + flip_chip(inc[1])
    for n in (0, 1):
        grad = finish_call(core_arg, plan[n][0], returned[n], control, grad)
    return jnp.transpose(inc, (1, 0, 2)), jnp.transpose(grad, (0, 2, 1, 3))


def solution(mesh):
    placed = (
        P(None, "lev", "tile", None),
        P(None, "lev", "tile", None),
        P("tile", None),
        P(),
        P(),
        P("tile", None),
        P("tile"),
        P("tile", None, "lev"),
    )
    return jax.shard_map(
        local,
        mesh=mesh,
        in_specs=placed,
        out_specs=(P("lev", "tile", None), P(None, "lev", "tile", None)),
        check_vma=False,
    )
```
